32 devices in a mesh: dp: 8 (over y, x, core), expert: 4 (over z).
Axes of the slice: x: 2, y: 2, z: 4, core: 2. Of those that a mesh axis runs over, the one named last changes fastest.
Arguments:
- tokens: bfloat16 [4096, 4096], P(('dp', 'expert')), may hold values from -6 to 6
- expert_ids: int32 [4096, 8], P(('dp', 'expert')), may hold values from 0 to 31, all different within a row; in each aligned block of 128 rows (0 to 127, 128 to 255, ...) at most 48 rows name the same one
- route_weight: float32 [4096, 8], P(('dp', 'expert')), may hold values from 0.05 to 1
- w_gate: bfloat16 [32, 4096, 768], P(('dp', 'expert')), may hold values from -0.09375 to 0.09375
- w_up: bfloat16 [32, 4096, 768], P(('dp', 'expert')), may hold values from -0.09375 to 0.09375
- w_down: bfloat16 [32, 768, 4096], P(('dp', 'expert')), may hold values from -0.21875 to 0.21875
Outputs:
- moe_out: bfloat16 [4096, 4096], P(('dp', 'expert'))
The draws below stay inside these ranges and needn't reach their ends.
Inputs may be any that keep to these rules, and one draw needn't show every extreme that they name: `expert_ids`: each row names 8 different experts; in the rows of one device no expert is named more than 48 times.
All inputs are finite; a program needn't handle non-finite values.
Results may differ from the reference program's by a relative error of at most 0.008.
Values may be sent and summed in bfloat16 or wider, within the bound.
A program may use at most 128 MiB of HBM per device.

```python
import math
import jax
import jax.numpy as jnp
import numpy as np
from jax import lax

D = 4096
FF = 768
TOPK = 8
TOK_DEV = 128
EXPERTS = 32
CAP = 48
TOKENS = 4096


def steps_of(stream_key, extent, split, low, high):
    gain, own = 1.0, jax.random.fold_in(stream_key, 6)
    for dim, shards_of in split:
        steps = jnp.exp(jax.random.uniform(jax.random.fold_in(own, dim), (shards_of,), jnp.float32, low / len(split), high / len(split)))
        gain = gain * jnp.repeat(steps, extent[dim] // shards_of).reshape([-1 if axis == dim else 1 for axis in range(len(extent))])
    return gain


def shared_out(rng, own, number, rows, number_of, top, most, slope):
    order = jax.random.permutation(rng, number_of)
    heavy_load, usual = portions_of(number_of, rows * top, most, slope, True), portions_of(number_of, rows * top, most, slope, False)
    places = jnp.arange(number_of)

    def named(lengths, turn):
        used = int((lengths > 0).sum())
        fixed = max(1, used // 4)
        passed = fixed + (places - fixed + turn * (used - fixed)) % max(1, number_of - fixed)
        return jnp.zeros((number_of,), jnp.int32).at[order[jnp.where(places < fixed, places, passed)]].set(jnp.asarray(lengths, jnp.int32))

    lengths = jnp.where(number % 4 == 0, named(heavy_load, number // 4), named(usual, number - number // 4 - 1))
    mixed = jax.random.permutation(jax.random.fold_in(own, 3), number_of)
    source_of, receiver = mixed[0:number_of // 2 * 2:2], mixed[1:number_of // 2 * 2:2]
    margin = jnp.minimum(lengths[source_of] - 1, most - lengths[receiver]) // 2
    margin = jnp.where((source_of == order[0]) | (receiver == order[0]) | (lengths[receiver] == 0), 0, jnp.maximum(margin, 0))
    passed = jax.random.randint(jax.random.fold_in(own, 4), (number_of // 2,), 0, 1 << 20) % (margin + 1)
    lengths = lengths.at[source_of].add(-passed).at[receiver].add(passed)
    labels = jnp.searchsorted(jnp.cumsum(lengths), jnp.arange(rows * top), side="right").astype(jnp.int32)
    table = labels.reshape(top, rows).T
    table = table[jax.random.permutation(jax.random.fold_in(own, 1), rows)]
    turn = jax.random.randint(jax.random.fold_in(own, 2), (rows, 1), 0, top)
    return jnp.take_along_axis(table, (jnp.arange(top)[None, :] + turn) % top, axis=1)


def portions_of(count, total, most, slope, full):
    loads = [(1 << 20) // math.isqrt(rank ** slope) + 1 for rank in range(1, count + 1)]
    largest = most if full else min(most, max(-(-total // count), total * loads[0] // sum(loads)))
    least = 1 if total - largest >= count - 1 else 0
    holding, surplus = [largest] + [least] * (count - 1), total - largest - least * (count - 1)
    while surplus > 0:
        movable = [i for i in range(1, count) if holding[i] < largest] or [i for i in range(1, count) if holding[i] < most]
        mass, budget = sum([loads[i] for i in movable]), surplus
        for i in movable:
            more = min(most - holding[i], max(1, budget * loads[i] // mass), surplus)
            holding[i] = holding[i] + more
            surplus = surplus - more
    return np.array(holding)


def noise(rng, shape, deviation, most, pieces=(), kind=jnp.bfloat16):
    array = deviation * jax.random.normal(rng, shape, jnp.float32)
    if pieces:
        array = array * steps_of(rng, shape, pieces, -0.22, 0.18)
    return jnp.clip(array, -most, most).astype(kind)


def setup_inputs(seed: int = 0) -> dict:
    seeds = jax.random.split(jax.random.key(seed), 7)
    tokens = noise(seeds[0], (TOKENS, D), 1.0, 6.0, ((0, 32),))
    expert_ids_keys = jax.random.split(jax.random.fold_in(seeds[1], 1), TOKENS // TOK_DEV)
    expert_ids_turns = jax.random.permutation(jax.random.fold_in(seeds[1], 3), TOKENS // TOK_DEV)
    expert_ids = jax.vmap(lambda own, number: shared_out(jax.random.fold_in(seeds[1], 2), own, number, TOK_DEV, EXPERTS, TOPK, CAP, 2))(expert_ids_keys, expert_ids_turns).reshape((TOKENS, TOPK))
    route_weight = jnp.clip(jnp.exp(math.log(1.0) - 2.9957323 * jax.random.uniform(seeds[2], (TOKENS, TOPK), jnp.float32) ** steps_of(seeds[2], (TOKENS, TOPK), ((0, 32),), -0.2, 0.2)), 0.05, 1.0)
    w_gate = noise(seeds[3], (EXPERTS, D, FF), D ** -0.5, 0.09375, ((0, 32),))
    w_up = noise(seeds[4], (EXPERTS, D, FF), D ** -0.5, 0.09375, ((0, 32),))
    w_down = noise(seeds[5], (EXPERTS, FF, D), FF ** -0.5, 0.21875, ((0, 32),))
    return {"tokens": tokens, "expert_ids": expert_ids, "route_weight": route_weight, "w_gate": w_gate, "w_up": w_up, "w_down": w_down}


def reference(tokens, expert_ids, route_weight, w_gate, w_up, w_down):
    flat_ids = expert_ids.reshape(-1).astype(jnp.int32)
    flat_weight = route_weight.reshape(-1)
    limit = EXPERTS * CAP

    def one_expert(total, expert):
        chosen = flat_ids == expert
        picked_rows = jnp.nonzero(chosen, size=limit, fill_value=0)[0].astype(jnp.int32)
        valid = jnp.arange(limit, dtype=jnp.int32) < jnp.sum(chosen.astype(jnp.int32))
        token_rows = (picked_rows // TOPK).astype(jnp.int32)
        arrived = tokens[token_rows]
        gate_act = jnp.dot(arrived, w_gate[expert], preferred_element_type=jnp.float32)
        up_act = jnp.dot(arrived, w_up[expert], preferred_element_type=jnp.float32)
        hidden = (jax.nn.silu(gate_act) * up_act).astype(jnp.bfloat16)
        projected = jnp.dot(hidden, w_down[expert], preferred_element_type=jnp.float32).astype(jnp.bfloat16)
        scale = jnp.where(valid, flat_weight[picked_rows], jnp.float32(0.0))
        term = projected.astype(jnp.float32) * scale[:, None]
        return total.at[token_rows].add(term), None

    start = jnp.zeros((TOKENS, D), jnp.float32)
    total = lax.scan(one_expert, start, jnp.arange(EXPERTS, dtype=jnp.int32))[0]
    return total.astype(jnp.bfloat16)
```

```python
import functools

import jax
import jax.numpy as jnp
from jax import lax
from jax.experimental import pallas as pl
from jax.experimental.pallas import tpu as pltpu
from jax.sharding import PartitionSpec as P

MESH = pl.DeviceIdType.MESH


def tile_of(extent, most):
    return most if extent % most == 0 else extent


def kernel(
    dp_count,
    ex_count,
    cap,
    tok_ref,
    wt_ref,
    wg_hbm,
    wu_hbm,
    wd_hbm,
    out_ref,
    zt,
    ret,
    wg,
    wu,
    wd,
    zw,
    tok,
    send,
    recv,
    hid,
    zret,
    weight_sem,
    local_sem,
    zt_send,
    zt_recv,
    zw_send,
    zw_recv,
    send_sem,
    recv_sem,
    back_send,
    back_recv,
    zret_send,
    zret_recv,
):
    p = lax.axis_index("dp")
    z = lax.axis_index("expert")
    width = tok_ref.shape[1]
    ff = wg.shape[1]
    tok_dev = tok_ref.shape[0]
    mine = pl.ds(pl.multiple_of(p * cap, cap), cap)
    others = pl.ds(0, (dp_count - 1) * cap)
    ff_tile = tile_of(ff, 256)
    col_tile = tile_of(width, 512)

    loads = [
        pltpu.make_async_copy(src, dst, weight_sem.at[i])
        for i, (src, dst) in enumerate(((wg_hbm, wg), (wu_hbm, wu), (wd_hbm, wd)))
    ]
    own = pltpu.make_async_copy(tok_ref, tok, local_sem.at[0])
    own.start()
    own_wt = pltpu.make_async_copy(wt_ref.at[z], zw.at[0], local_sem.at[1])
    own_wt.start()
    for load in loads:
        load.start()

    barrier = pltpu.get_barrier_semaphore()
    for d in range(1, dp_count):
        pl.semaphore_signal(barrier, inc=1, device_id=((p + d) % dp_count, z), device_id_type=MESH)
    for d in range(1, ex_count):
        pl.semaphore_signal(barrier, inc=1, device_id=(p, (z + d) % ex_count), device_id_type=MESH)
    pl.semaphore_wait(barrier, dp_count + ex_count - 2)

    def token_copy(d):
        return pltpu.make_async_remote_copy(
            src_ref=tok_ref,
            dst_ref=zt.at[d],
            send_sem=zt_send.at[d],
            recv_sem=zt_recv.at[d],
            device_id=(p, (z + d) % ex_count),
            device_id_type=MESH,
        )

    def table_copy(d):
        target = (z + d) % ex_count
        return pltpu.make_async_remote_copy(
            src_ref=wt_ref.at[target],
            dst_ref=zw.at[d],
            send_sem=zw_send.at[d],
            recv_sem=zw_recv.at[d],
            device_id=(p, target),
            device_id_type=MESH,
        )

    def partial_copy(t):
        return pltpu.make_async_remote_copy(
            src_ref=recv.at[t, pl.ds(0, tok_dev)],
            dst_ref=zret.at[t],
            send_sem=zret_send.at[t],
            recv_sem=zret_recv.at[t],
            device_id=(p, (z + ex_count - t) % ex_count),
            device_id_type=MESH,
        )

    def wait_for(ref, sem):
        pltpu.make_async_copy(ref, ref, sem).wait()

    for d in range(1, ex_count):
        table_copy(d).start()
        token_copy(d).start()

    def dispatch(t):
        slot = lax.rem(t, 2)
        table = (zw[t] > 0.0).astype(jnp.bfloat16)

        @pl.loop(0, width // col_tile)
        def _(i):
            cols = pl.ds(pl.multiple_of(i * col_tile, col_tile), col_tile)
            rows = jnp.dot(table, tok[:, cols], preferred_element_type=jnp.float32)
            send[slot, :, cols] = rows.astype(jnp.bfloat16)

        for d in range(1, dp_count):
            peer = (p + d) % dp_count
            pltpu.make_async_remote_copy(
                src_ref=send.at[slot, pl.ds(pl.multiple_of(peer * cap, cap), cap)],
                dst_ref=recv.at[t, mine],
                send_sem=send_sem.at[slot],
                recv_sem=recv_sem.at[t],
                device_id=(peer, z),
                device_id_type=MESH,
            ).start()
        keep = pltpu.make_async_copy(send.at[slot, mine], recv.at[t, mine], local_sem.at[0])
        keep.start()
        keep.wait()

    def arrived(t):
        token_copy(t).wait_recv()
        table_copy(t).wait_recv()
        load = pltpu.make_async_copy(zt.at[t], tok, local_sem.at[0])
        load.start()
        load.wait()

    def expert(t):
        wait_for(recv.at[t, others], recv_sem.at[t])

        @pl.loop(0, ff // ff_tile)
        def _(i):
            cols = pl.ds(pl.multiple_of(i * ff_tile, ff_tile), ff_tile)
            gate = jnp.dot(recv[t], wg[:, cols], preferred_element_type=jnp.float32)
            up = jnp.dot(recv[t], wu[:, cols], preferred_element_type=jnp.float32)
            hid[:, cols] = (gate / (1.0 + jnp.exp(-gate)) * up).astype(jnp.bfloat16)

        @pl.loop(0, width // col_tile)
        def _(i):
            cols = pl.ds(pl.multiple_of(i * col_tile, col_tile), col_tile)
            rows = jnp.dot(hid[...], wd[:, cols], preferred_element_type=jnp.float32)
            recv[t, :, cols] = rows.astype(jnp.bfloat16)

        for d in range(1, dp_count):
            peer = (p + d) % dp_count
            pltpu.make_async_remote_copy(
                src_ref=recv.at[t, pl.ds(pl.multiple_of(peer * cap, cap), cap)],
                dst_ref=ret.at[t, mine],
                send_sem=back_send.at[t],
                recv_sem=back_recv.at[t],
                device_id=(peer, z),
                device_id_type=MESH,
            ).start()
        keep = pltpu.make_async_copy(recv.at[t, mine], ret.at[t, mine], local_sem.at[0])
        keep.start()
        keep.wait()

    def combined(t, store):
        wait_for(ret.at[t, others], back_recv.at[t])
        load = pltpu.make_async_copy(ret.at[t], send.at[0], local_sem.at[0])
        load.start()
        wait_for(recv.at[t, others], back_send.at[t])
        load.wait()
        weight = zw[t].T
        high = weight.astype(jnp.bfloat16)
        low = (weight - high.astype(jnp.float32)).astype(jnp.bfloat16)

        @pl.loop(0, width // col_tile)
        def _(i):
            cols = pl.ds(pl.multiple_of(i * col_tile, col_tile), col_tile)
            rows = send[0, :, cols]
            total = jnp.dot(high, rows, preferred_element_type=jnp.float32)
            total = total + jnp.dot(low, rows, preferred_element_type=jnp.float32)
            store(cols, total)

    own.wait()
    own_wt.wait()
    dispatch(0)
    arrived(1)
    dispatch(1)
    for load in loads:
        load.wait()

    def middle(t, carry):
        arrived(t)
        wait_for(send.at[lax.rem(t, 2), others], send_sem.at[lax.rem(t, 2)])
        dispatch(t)
        expert(t - 1)
        return carry

    lax.fori_loop(2, ex_count, middle, 0)

    def last(t, carry):
        expert(lax.rem(t, ex_count))
        return carry

    lax.fori_loop(ex_count - 1, ex_count + 1, last, 0)
    for slot in range(2):
        wait_for(send.at[slot, others], send_sem.at[slot])

    def home(t, carry):
        def store(cols, total):
            recv[t, pl.ds(0, tok_dev), cols] = total.astype(jnp.bfloat16)

        combined(t, store)
        partial_copy(t).start()
        return carry

    lax.fori_loop(1, ex_count, home, 0)

    for d in range(1, ex_count):
        partial_copy(d).wait_recv()

    def finish(cols, total):
        for d in range(1, ex_count):
            total = total + zret[d, :, cols].astype(jnp.float32)
        out_ref[:, cols] = total.astype(jnp.bfloat16)

    combined(0, finish)

    for d in range(1, ex_count):
        token_copy(d).wait_send()
        table_copy(d).wait_send()
        partial_copy(d).wait_send()


def body(tokens, expert_ids, route_weight, w_gate, w_up, w_down):
    tok_dev, width = tokens.shape
    top_count = expert_ids.shape[1]
    ff = w_gate.shape[2]
    dp_count = lax.axis_size("dp")
    ex_count = lax.axis_size("expert")
    experts = dp_count * ex_count
    needed = tok_dev * top_count * 3 // (2 * experts)
    cap = -(-needed // 16) * 16
    rows = dp_count * cap

    named = expert_ids.T[None, :, :] == jnp.arange(experts, dtype=jnp.int32)[:, None, None]
    chosen = jnp.any(named, axis=1)
    weight = jnp.sum(jnp.where(named, route_weight.T[None, :, :], 0.0), axis=1)
    index = jnp.arange(tok_dev, dtype=jnp.int32)
    before = (index[:, None] < index[None, :]).astype(jnp.bfloat16)
    slot = jnp.dot(chosen.astype(jnp.bfloat16), before, preferred_element_type=jnp.float32)
    slot = jnp.where(chosen, slot.astype(jnp.int32), -1)

    def by_plane(v):
        return v.reshape(dp_count, ex_count, 1, tok_dev).transpose(1, 0, 2, 3)

    at_slot = by_plane(slot) == jnp.arange(cap, dtype=jnp.int32)[None, None, :, None]
    table = jnp.where(at_slot, by_plane(weight), 0.0).reshape(ex_count, rows, tok_dev)

    any_space = pl.BlockSpec(memory_space=pl.ANY)
    vmem = pl.BlockSpec(memory_space=pltpu.VMEM)
    dma = pltpu.SemaphoreType.DMA
    out, _, _ = pl.pallas_call(
        functools.partial(kernel, dp_count, ex_count, cap),
        out_shape=(
            jax.ShapeDtypeStruct((tok_dev, width), jnp.bfloat16),
            jax.ShapeDtypeStruct((ex_count, tok_dev, width), jnp.bfloat16),
            jax.ShapeDtypeStruct((ex_count, rows, width), jnp.bfloat16),
        ),
        in_specs=[any_space, any_space, any_space, any_space, any_space],
        out_specs=(vmem, any_space, any_space),
        scratch_shapes=[
            pltpu.VMEM((width, ff), jnp.bfloat16),
            pltpu.VMEM((width, ff), jnp.bfloat16),
            pltpu.VMEM((ff, width), jnp.bfloat16),
            pltpu.VMEM((ex_count, rows, tok_dev), jnp.float32),
            pltpu.VMEM((tok_dev, width), jnp.bfloat16),
            pltpu.VMEM((2, rows, width), jnp.bfloat16),
            pltpu.VMEM((ex_count, rows, width), jnp.bfloat16),
            pltpu.VMEM((rows, ff), jnp.bfloat16),
            pltpu.VMEM((ex_count, tok_dev, width), jnp.bfloat16),
            dma((3,)),
            dma((2,)),
            dma((ex_count,)),
            dma((ex_count,)),
            dma((ex_count,)),
            dma((ex_count,)),
            dma((2,)),
            dma((ex_count,)),
            dma((ex_count,)),
            dma((ex_count,)),
            dma((ex_count,)),
            dma((ex_count,)),
        ],
        compiler_params=pltpu.CompilerParams(
            collective_id=0, has_side_effects=True, vmem_limit_bytes=60 * 1024 * 1024
        ),
        cost_estimate=pl.CostEstimate(
            flops=6 * ex_count * rows * width * ff,
            bytes_accessed=6 * width * ff + 6 * ex_count * rows * width,
            transcendentals=ex_count * rows * ff,
        ),
    )(tokens, table, w_gate[0], w_up[0], w_down[0])
    return out


def solution(mesh):
    placed = (
        P(("dp", "expert"), None),
        P(("dp", "expert"), None),
        P(("dp", "expert"), None),
        P(("dp", "expert"), None, None),
        P(("dp", "expert"), None, None),
        P(("dp", "expert"), None, None),
    )
    return jax.shard_map(
        body, mesh=mesh, in_specs=placed, out_specs=P(("dp", "expert"), None), check_vma=False
    )
```

```python
import functools

import jax
import jax.numpy as jnp
from jax import lax
from jax.experimental import pallas as pl
from jax.experimental.pallas import tpu as pltpu
from jax.sharding import PartitionSpec as P

MESH = pl.DeviceIdType.MESH


def tile_of(extent, most):
    return most if extent % most == 0 else extent


def kernel(
    dp_count,
    ex_count,
    cap,
    tok_ref,
    meta_ref,
    wg_hbm,
    wu_hbm,
    wd_hbm,
    out_ref,
    zt,
    xt,
    ret,
    wg,
    wu,
    wd,
    zm,
    xm,
    pick,
    share,
    tok,
    send,
    recv,
    hid,
    pret,
    zret,
    weight_sem,
    local_sem,
    zt_send,
    zt_recv,
    zm_send,
    zm_recv,
    xt_send,
    xt_recv,
    xm_send,
    xm_recv,
    send_sem,
    recv_sem,
    back_send,
    back_recv,
    pret_send,
    pret_recv,
    zret_send,
    zret_recv,
):
    p = lax.axis_index("dp")
    z = lax.axis_index("expert")
    group = dp_count // 4
    c = p % group
    b = (p // group) % 2
    a = p // (2 * group)
    odd = c % 2

    def device(row, column, member):
        return (row * 2 + column) * group + member

    first = device(a + odd * (1 - 2 * a), b + (1 - odd) * (1 - 2 * b), c)
    row2, column2 = a + (1 - odd) * (1 - 2 * a), b + odd * (1 - 2 * b)
    width = tok_ref.shape[1]
    ff = wg.shape[1]
    tok_dev = tok_ref.shape[0]
    part = 2 * cap
    others = pl.ds(0, (2 * group - 1) * part)
    ff_tile = tile_of(ff, 256)
    col_tile = tile_of(width, 512)

    def section(i):
        return pl.ds(pl.multiple_of(i * part, part), part)

    loads = [
        pltpu.make_async_copy(src, dst, weight_sem.at[i])
        for i, (src, dst) in enumerate(((wg_hbm, wg), (wu_hbm, wu), (wd_hbm, wd)))
    ]
    own = pltpu.make_async_copy(tok_ref, tok.at[pl.ds(0, tok_dev)], local_sem.at[0])
    own.start()
    own_meta = pltpu.make_async_copy(meta_ref.at[z], zm.at[0], local_sem.at[1])
    own_meta.start()
    for load in loads:
        load.start()

    barrier = pltpu.get_barrier_semaphore()
    for d in range(1, dp_count):
        pl.semaphore_signal(barrier, inc=1, device_id=((p + d) % dp_count, z), device_id_type=MESH)
    for d in range(1, ex_count):
        pl.semaphore_signal(barrier, inc=1, device_id=(p, (z + d) % ex_count), device_id_type=MESH)
    pick[...] = jnp.zeros_like(pick)
    share[...] = jnp.zeros_like(share)
    pl.semaphore_wait(barrier, dp_count + ex_count - 2)

    def remote(src, dst, send_at, recv_at, target):
        return pltpu.make_async_remote_copy(
            src_ref=src,
            dst_ref=dst,
            send_sem=send_at,
            recv_sem=recv_at,
            device_id=target,
            device_id_type=MESH,
        )

    def token_copy(d):
        return remote(
            tok_ref, zt.at[d], zt_send.at[d], zt_recv.at[d], (p, (z + d) % ex_count)
        )

    def meta_copy(d):
        target = (z + d) % ex_count
        return remote(meta_ref.at[target], zm.at[d], zm_send.at[d], zm_recv.at[d], (p, target))

    def pair_token_copy(t, src):
        return remote(src, xt.at[t], xt_send.at[t], xt_recv.at[t], (first, z))

    def pair_meta_copy(t):
        return remote(zm.at[t, 1], xm.at[t], xm_send.at[t], xm_recv.at[t], (first, z))

    def pair_partial_copy(t):
        return remote(
            recv.at[t, pl.ds(0, tok_dev)], pret.at[t], pret_send.at[t], pret_recv.at[t], (first, z)
        )

    def plane_partial_copy(t):
        return remote(
            recv.at[t, pl.ds(tok_dev, tok_dev)],
            zret.at[t - 1],
            zret_send.at[t],
            zret_recv.at[t],
            (p, (z + ex_count - t) % ex_count),
        )

    def wait_for(ref, sem):
        pltpu.make_async_copy(ref, ref, sem).wait()

    pair_token_copy(0, tok_ref).start()
    for d in range(1, ex_count):
        meta_copy(d).start()
        token_copy(d).start()
    own_meta.wait()
    pair_meta_copy(0).start()

    def exchange(t):
        meta_copy(t).wait_recv()
        pair_meta_copy(t).start()
        token_copy(t).wait_recv()
        pair_token_copy(t, zt.at[t]).start()

    def one_hot(meta, dest, value):
        slots = lax.broadcasted_iota(jnp.int32, (cap, tok_dev), 0).astype(jnp.float32)
        return jnp.where(meta[dest : dest + 1, :] == slots, value, 0.0)

    def dispatch(t, src):
        load = pltpu.make_async_copy(src, tok.at[pl.ds(0, tok_dev)], local_sem.at[0])
        load.start()
        pair_meta_copy(t).wait_recv()
        for block, meta in enumerate((zm[t, 0], xm[t])):
            for dest in range(2 * group):
                rows = pl.ds((2 * dest + block) * cap, cap)
                hot = one_hot(meta, dest, 1.0).astype(jnp.bfloat16)
                pick[rows, pl.ds(block * tok_dev, tok_dev)] = hot
        pair_token_copy(t, src).wait_recv()
        pair = pltpu.make_async_copy(xt.at[t], tok.at[pl.ds(tok_dev, tok_dev)], local_sem.at[1])
        pair.start()
        load.wait()
        pair.wait()
        slot = lax.rem(t, 2)

        @pl.loop(0, width // col_tile)
        def _(i):
            cols = pl.ds(pl.multiple_of(i * col_tile, col_tile), col_tile)
            rows = jnp.dot(pick[...], tok[:, cols], preferred_element_type=jnp.float32)
            send[slot, :, cols] = rows.astype(jnp.bfloat16)

        def give(dest, at, target):
            remote(
                send.at[slot, section(dest)],
                recv.at[t, section(at)],
                send_sem.at[slot],
                recv_sem.at[t],
                (target, z),
            ).start()

        for member in range(group):
            give(group + member, group + c, device(row2, column2, member))
        for d in range(1, group):
            member = (c + d) % group
            give(member, c, device(a, b, member))
        keep = pltpu.make_async_copy(
            send.at[slot, section(c)], recv.at[t, section(c)], local_sem.at[0]
        )
        keep.start()
        keep.wait()

    def expert(t):
        wait_for(recv.at[t, others], recv_sem.at[t])

        @pl.loop(0, ff // ff_tile)
        def _(i):
            cols = pl.ds(pl.multiple_of(i * ff_tile, ff_tile), ff_tile)
            gate = jnp.dot(recv[t], wg[:, cols], preferred_element_type=jnp.float32)
            up = jnp.dot(recv[t], wu[:, cols], preferred_element_type=jnp.float32)
            hid[:, cols] = (gate / (1.0 + jnp.exp(-gate)) * up).astype(jnp.bfloat16)

        @pl.loop(0, width // col_tile)
        def _(i):
            cols = pl.ds(pl.multiple_of(i * col_tile, col_tile), col_tile)
            rows = jnp.dot(hid[...], wd[:, cols], preferred_element_type=jnp.float32)
            recv[t, :, cols] = rows.astype(jnp.bfloat16)

        def give_back(at, dest, target):
            remote(
                recv.at[t, section(at)],
                ret.at[t, section(dest)],
                back_send.at[t],
                back_recv.at[t],
                (target, z),
            ).start()

        for member in range(group):
            target = device(1 - a, b, member) if member % 2 == 0 else device(a, 1 - b, member)
            give_back(group + member, group + c, target)
        for d in range(1, group):
            member = (c + d) % group
            give_back(member, c, device(a, b, member))
        keep = pltpu.make_async_copy(
            recv.at[t, section(c)], ret.at[t, section(c)], local_sem.at[0]
        )
        keep.start()
        keep.wait()

    def weighted(t, block, store):
        meta = xm[t] if block else zm[t, 0]
        for dest in range(2 * group):
            weight = meta[2 * group + dest : 2 * group + dest + 1, :]
            rows = pl.ds((2 * dest + block) * cap, cap)
            share[block, rows, :] = one_hot(meta, dest, weight)
        weight = share[block].T
        high = weight.astype(jnp.bfloat16)
        low = (weight - high.astype(jnp.float32)).astype(jnp.bfloat16)

        @pl.loop(0, width // col_tile)
        def _(i):
            cols = pl.ds(pl.multiple_of(i * col_tile, col_tile), col_tile)
            rows = send[0, :, cols]
            total = jnp.dot(high, rows, preferred_element_type=jnp.float32)
            total = total + jnp.dot(low, rows, preferred_element_type=jnp.float32)
            store(cols, total)

    def combined(t, store):
        wait_for(ret.at[t, others], back_recv.at[t])
        load = pltpu.make_async_copy(ret.at[t], send.at[0], local_sem.at[0])
        load.start()
        wait_for(recv.at[t, others], back_send.at[t])
        load.wait()

        def store_pair(cols, total):
            recv[t, pl.ds(0, tok_dev), cols] = total.astype(jnp.bfloat16)

        weighted(t, 1, store_pair)
        pair_partial_copy(t).start()
        pair_partial_copy(t).wait_recv()
        weighted(t, 0, store)

    own.wait()
    dispatch(0, tok_ref)
    exchange(1)
    dispatch(1, zt.at[1])
    for load in loads:
        load.wait()

    def reuse(t):
        wait_for(send.at[lax.rem(t, 2), others], send_sem.at[lax.rem(t, 2)])

    exchange(2)
    expert(1)
    reuse(2)
    dispatch(2, zt.at[2])

    def middle(t, carry):
        exchange(t)
        reuse(t)
        dispatch(t, zt.at[t])
        expert(t - 1)
        return carry

    lax.fori_loop(3, ex_count, middle, 0)

    def last(t, carry):
        expert(lax.rem(t, ex_count))
        return carry

    lax.fori_loop(ex_count - 1, ex_count + 1, last, 0)
    for slot in range(2):
        wait_for(send.at[slot, others], send_sem.at[slot])

    def home(t, carry):
        def store(cols, total):
            total = total + pret[t, :, cols].astype(jnp.float32)
            recv[t, pl.ds(tok_dev, tok_dev), cols] = total.astype(jnp.bfloat16)

        combined(t, store)
        plane_partial_copy(t).start()
        return carry

    lax.fori_loop(1, ex_count, home, 0)

    def finish(cols, total):
        total = total + pret[0, :, cols].astype(jnp.float32)
        out_ref[:, cols] = total.astype(jnp.bfloat16)

    def finish_all(cols, total):
        for d in range(1, ex_count):
            total = total + zret[d - 1, :, cols].astype(jnp.float32)
        finish(cols, total)

    for d in range(1, ex_count):
        plane_partial_copy(d).wait_recv()
    combined(0, finish_all)

    pair_token_copy(0, tok_ref).wait_send()
    pair_meta_copy(0).wait_send()
    pair_partial_copy(0).wait_send()
    for d in range(1, ex_count):
        token_copy(d).wait_send()
        meta_copy(d).wait_send()
        pair_token_copy(d, zt.at[d]).wait_send()
        pair_meta_copy(d).wait_send()
        pair_partial_copy(d).wait_send()
        plane_partial_copy(d).wait_send()


def body(tokens, expert_ids, route_weight, w_gate, w_up, w_down):
    tok_dev, width = tokens.shape
    top_count = expert_ids.shape[1]
    ff = w_gate.shape[2]
    dp_count = lax.axis_size("dp")
    ex_count = lax.axis_size("expert")
    experts = dp_count * ex_count
    group = dp_count // 4
    needed = tok_dev * top_count * 3 // (2 * experts)
    cap = -(-needed // 16) * 16
    rows = dp_count * cap

    named = expert_ids.T[None, :, :] == jnp.arange(experts, dtype=jnp.int32)[:, None, None]
    chosen = jnp.any(named, axis=1)
    weight = jnp.sum(jnp.where(named, route_weight.T[None, :, :], 0.0), axis=1)
    index = jnp.arange(tok_dev, dtype=jnp.int32)
    before = (index[:, None] < index[None, :]).astype(jnp.bfloat16)
    slot = jnp.dot(chosen.astype(jnp.bfloat16), before, preferred_element_type=jnp.float32)
    slot = jnp.where(chosen, slot, -1.0)

    p = lax.axis_index("dp")
    c, b, a = p % group, (p // group) % 2, p // (2 * group)
    even = c % 2 == 0
    sides = []
    for side in range(2):
        for other in range(2):
            row = jnp.where(even, (a + other) % 2, (a + side) % 2)
            column = jnp.where(even, (b + side) % 2, (b + other) % 2)
            sides.append((row * 2 + column) * group + jnp.arange(group))
    order = jnp.concatenate(sides)

    def by_plane(v):
        v = v.reshape(dp_count, ex_count, tok_dev)[order]
        return v.reshape(2, 2 * group, ex_count, tok_dev).transpose(2, 0, 1, 3)

    meta = jnp.concatenate([by_plane(slot), by_plane(weight)], axis=2)

    any_space = pl.BlockSpec(memory_space=pl.ANY)
    vmem = pl.BlockSpec(memory_space=pltpu.VMEM)
    dma = pltpu.SemaphoreType.DMA
    each = dma((ex_count,))
    out, _, _, _ = pl.pallas_call(
        functools.partial(kernel, dp_count, ex_count, cap),
        out_shape=(
            jax.ShapeDtypeStruct((tok_dev, width), jnp.bfloat16),
            jax.ShapeDtypeStruct((ex_count, tok_dev, width), jnp.bfloat16),
            jax.ShapeDtypeStruct((ex_count, tok_dev, width), jnp.bfloat16),
            jax.ShapeDtypeStruct((ex_count, rows, width), jnp.bfloat16),
        ),
        in_specs=[any_space, any_space, any_space, any_space, any_space],
        out_specs=(vmem, any_space, any_space, any_space),
        scratch_shapes=[
            pltpu.VMEM((width, ff), jnp.bfloat16),
            pltpu.VMEM((width, ff), jnp.bfloat16),
            pltpu.VMEM((ff, width), jnp.bfloat16),
            pltpu.VMEM((ex_count, 2, 4 * group, tok_dev), jnp.float32),
            pltpu.VMEM((ex_count, 4 * group, tok_dev), jnp.float32),
            pltpu.VMEM((rows, 2 * tok_dev), jnp.bfloat16),
            pltpu.VMEM((2, rows, tok_dev), jnp.float32),
            pltpu.VMEM((2 * tok_dev, width), jnp.bfloat16),
            pltpu.VMEM((2, rows, width), jnp.bfloat16),
            pltpu.VMEM((ex_count, rows, width), jnp.bfloat16),
            pltpu.VMEM((rows, ff), jnp.bfloat16),
            pltpu.VMEM((ex_count, tok_dev, width), jnp.bfloat16),
            pltpu.VMEM((ex_count - 1, tok_dev, width), jnp.bfloat16),
            dma((3,)),
            dma((2,)),
            each,
            each,
            each,
            each,
            each,
            each,
            each,
            each,
            dma((2,)),
            each,
            each,
            each,
            each,
            each,
            each,
            each,
        ],
        compiler_params=pltpu.CompilerParams(
            collective_id=0, has_side_effects=True, vmem_limit_bytes=60 * 1024 * 1024
        ),
        cost_estimate=pl.CostEstimate(
            flops=6 * ex_count * rows * width * ff,
            bytes_accessed=6 * width * ff + 6 * ex_count * rows * width,
            transcendentals=ex_count * rows * ff,
        ),
    )(tokens, meta, w_gate[0], w_up[0], w_down[0])
    return out


def solution(mesh):
    placed = (
        P(("dp", "expert"), None),
        P(("dp", "expert"), None),
        P(("dp", "expert"), None),
        P(("dp", "expert"), None, None),
        P(("dp", "expert"), None, None),
        P(("dp", "expert"), None, None),
    )
    return jax.shard_map(
        body, mesh=mesh, in_specs=placed, out_specs=P(("dp", "expert"), None), check_vma=False
    )
```

```python
import functools

import jax
import jax.numpy as jnp
from jax import lax
from jax.experimental import pallas as pl
from jax.experimental.pallas import tpu as pltpu
from jax.sharding import PartitionSpec as P

MESH = pl.DeviceIdType.MESH


def tile_of(extent, most):
    return most if extent % most == 0 else extent


def kernel(
    dp_count,
    ex_count,
    cap,
    tok_ref,
    meta_ref,
    wg_hbm,
    wu_hbm,
    wd_hbm,
    out_ref,
    zt,
    xt,
    ret,
    wg,
    wu,
    wd,
    zm,
    xm,
    pick,
    share,
    tok,
    send,
    recv,
    hid,
    pret,
    zret,
    weight_sem,
    local_sem,
    zt_send,
    zt_recv,
    zm_send,
    zm_recv,
    xt_send,
    xt_recv,
    xm_send,
    xm_recv,
    send_sem,
    recv_sem,
    back_send,
    back_recv,
    pret_send,
    pret_recv,
    zret_send,
    zret_recv,
):
    p = lax.axis_index("dp")
    z = lax.axis_index("expert")
    group = dp_count // 4
    c = p % group
    b = (p // group) % 2
    a = p // (2 * group)
    odd = c % 2

    def device(row, column, member):
        return (row * 2 + column) * group + member

    first = device(a + odd * (1 - 2 * a), b + (1 - odd) * (1 - 2 * b), c)
    row2, column2 = a + (1 - odd) * (1 - 2 * a), b + odd * (1 - 2 * b)
    width = tok_ref.shape[1]
    ff = wg.shape[1]
    tok_dev = tok_ref.shape[0]
    part = 2 * cap
    others = pl.ds(0, (2 * group - 1) * part)
    ff_tile = tile_of(ff, 256)
    col_tile = tile_of(width, 512)

    def section(i):
        return pl.ds(pl.multiple_of(i * part, part), part)

    loads = [
        pltpu.make_async_copy(src, dst, weight_sem.at[i])
        for i, (src, dst) in enumerate(((wg_hbm, wg), (wu_hbm, wu), (wd_hbm, wd)))
    ]
    own = pltpu.make_async_copy(tok_ref, tok.at[pl.ds(0, tok_dev)], local_sem.at[0])
    own.start()
    own_meta = pltpu.make_async_copy(meta_ref.at[z], zm.at[z], local_sem.at[1])
    own_meta.start()
    for load in loads:
        load.start()

    barrier = pltpu.get_barrier_semaphore()
    for d in range(1, dp_count):
        pl.semaphore_signal(barrier, inc=1, device_id=((p + d) % dp_count, z), device_id_type=MESH)
    for d in range(1, ex_count):
        pl.semaphore_signal(barrier, inc=1, device_id=(p, (z + d) % ex_count), device_id_type=MESH)
    pick[...] = jnp.zeros_like(pick)
    share[...] = jnp.zeros_like(share)
    pl.semaphore_wait(barrier, dp_count + ex_count - 2)

    def remote(src, dst, send_at, recv_at, target):
        return pltpu.make_async_remote_copy(
            src_ref=src,
            dst_ref=dst,
            send_sem=send_at,
            recv_sem=recv_at,
            device_id=target,
            device_id_type=MESH,
        )

    low_half = 2 * z <= ex_count - 1
    paired = jnp.where(low_half, 2 * z, 2 * (ex_count - 1 - z))

    def source(t):
        near = jnp.where(t % 2 == 1, z - (t + 1) // 2, z + t // 2)
        return jnp.where(t <= paired, near, jnp.where(low_half, t, ex_count - 1 - t))

    has_up, has_down = z + 1 < ex_count, z >= 1

    def up_copy(src, s):
        return remote(src, zt.at[s], zt_send.at[s], zt_recv.at[s], (p, (z + 1) % ex_count))

    def down_copy(src, s, at):
        target = (p, (z + ex_count - 1) % ex_count)
        return remote(src, zt.at[s], zt_send.at[at], zt_recv.at[s], target)

    def passed_on(s, act):
        @pl.when(jnp.logical_and(s < z, has_up))
        def _():
            act(up_copy(zt.at[s], s))

        @pl.when(jnp.logical_and(s > z, has_down))
        def _():
            act(down_copy(zt.at[s], s, s))

    def sent_out(act):
        @pl.when(has_up)
        def _():
            act(up_copy(tok_ref, z))

        @pl.when(has_down)
        def _():
            act(down_copy(tok_ref, z, ex_count))

    def meta_copy(d):
        target = (z + d) % ex_count
        return remote(meta_ref.at[target], zm.at[z], zm_send.at[d], zm_recv.at[z], (p, target))

    def pair_token_copy(t, src):
        return remote(src, xt.at[t], xt_send.at[t], xt_recv.at[t], (first, z))

    def pair_meta_copy(t):
        return remote(zm.at[source(t), 1], xm.at[t], xm_send.at[t], xm_recv.at[t], (first, z))

    def pair_partial_copy(t):
        return remote(
            recv.at[t, pl.ds(0, tok_dev)], pret.at[t], pret_send.at[t], pret_recv.at[t], (first, z)
        )

    def plane_partial_copy(t):
        s = source(t)
        away = (z + ex_count - s) % ex_count
        return remote(
            recv.at[t, pl.ds(tok_dev, tok_dev)],
            zret.at[away - 1],
            zret_send.at[t],
            zret_recv.at[away],
            (p, s),
        )

    def wait_for(ref, sem):
        pltpu.make_async_copy(ref, ref, sem).wait()

    sent_out(lambda copy: copy.start())
    pair_token_copy(0, tok_ref).start()
    for d in range(1, ex_count):
        meta_copy(d).start()
    own_meta.wait()
    pair_meta_copy(0).start()

    def exchange(t):
        s = source(t)
        wait_for(zm.at[s], zm_recv.at[s])
        pair_meta_copy(t).start()
        wait_for(zt.at[s], zt_recv.at[s])
        passed_on(s, lambda copy: copy.start())
        pair_token_copy(t, zt.at[s]).start()

    def one_hot(meta, dest, value):
        slots = lax.broadcasted_iota(jnp.int32, (cap, tok_dev), 0).astype(jnp.float32)
        return jnp.where(meta[dest : dest + 1, :] == slots, value, 0.0)

    def dispatch(t, src):
        load = pltpu.make_async_copy(src, tok.at[pl.ds(0, tok_dev)], local_sem.at[0])
        load.start()
        pair_meta_copy(t).wait_recv()
        for block, meta in enumerate((zm[source(t), 0], xm[t])):
            for dest in range(2 * group):
                rows = pl.ds((2 * dest + block) * cap, cap)
                hot = one_hot(meta, dest, 1.0).astype(jnp.bfloat16)
                pick[rows, pl.ds(block * tok_dev, tok_dev)] = hot
        pair_token_copy(t, src).wait_recv()
        pair = pltpu.make_async_copy(xt.at[t], tok.at[pl.ds(tok_dev, tok_dev)], local_sem.at[1])
        pair.start()
        load.wait()
        pair.wait()
        slot = lax.rem(t, 2)

        @pl.loop(0, width // col_tile)
        def _(i):
            cols = pl.ds(pl.multiple_of(i * col_tile, col_tile), col_tile)
            rows = jnp.dot(pick[...], tok[:, cols], preferred_element_type=jnp.float32)
            send[slot, :, cols] = rows.astype(jnp.bfloat16)

        def give(dest, at, target):
            remote(
                send.at[slot, section(dest)],
                recv.at[t, section(at)],
                send_sem.at[slot],
                recv_sem.at[t],
                (target, z),
            ).start()

        for member in range(group):
            give(group + member, group + c, device(row2, column2, member))
        for d in range(1, group):
            member = (c + d) % group
            give(member, c, device(a, b, member))
        keep = pltpu.make_async_copy(
            send.at[slot, section(c)], recv.at[t, section(c)], local_sem.at[0]
        )
        keep.start()
        keep.wait()

    def expert(t):
        wait_for(recv.at[t, others], recv_sem.at[t])

        @pl.loop(0, ff // ff_tile)
        def _(i):
            cols = pl.ds(pl.multiple_of(i * ff_tile, ff_tile), ff_tile)
            gate = jnp.dot(recv[t], wg[:, cols], preferred_element_type=jnp.float32)
            up = jnp.dot(recv[t], wu[:, cols], preferred_element_type=jnp.float32)
            hid[:, cols] = (gate / (1.0 + jnp.exp(-gate)) * up).astype(jnp.bfloat16)

        @pl.loop(0, width // col_tile)
        def _(i):
            cols = pl.ds(pl.multiple_of(i * col_tile, col_tile), col_tile)
            rows = jnp.dot(hid[...], wd[:, cols], preferred_element_type=jnp.float32)
            recv[t, :, cols] = rows.astype(jnp.bfloat16)

        def give_back(at, dest, target):
            remote(
                recv.at[t, section(at)],
                ret.at[t, section(dest)],
                back_send.at[t],
                back_recv.at[t],
                (target, z),
            ).start()

        for member in range(group):
            target = device(1 - a, b, member) if member % 2 == 0 else device(a, 1 - b, member)
            give_back(group + member, group + c, target)
        for d in range(1, group):
            member = (c + d) % group
            give_back(member, c, device(a, b, member))
        keep = pltpu.make_async_copy(
            recv.at[t, section(c)], ret.at[t, section(c)], local_sem.at[0]
        )
        keep.start()
        keep.wait()

    def weighted(t, block, store):
        meta = xm[t] if block else zm[source(t), 0]
        for dest in range(2 * group):
            weight = meta[2 * group + dest : 2 * group + dest + 1, :]
            rows = pl.ds((2 * dest + block) * cap, cap)
            share[block, rows, :] = one_hot(meta, dest, weight)
        weight = share[block].T
        high = weight.astype(jnp.bfloat16)
        low = (weight - high.astype(jnp.float32)).astype(jnp.bfloat16)

        @pl.loop(0, width // col_tile)
        def _(i):
            cols = pl.ds(pl.multiple_of(i * col_tile, col_tile), col_tile)
            rows = send[0, :, cols]
            total = jnp.dot(high, rows, preferred_element_type=jnp.float32)
            total = total + jnp.dot(low, rows, preferred_element_type=jnp.float32)
            store(cols, total)

    def combined(t, store):
        wait_for(ret.at[t, others], back_recv.at[t])
        load = pltpu.make_async_copy(ret.at[t], send.at[0], local_sem.at[0])
        load.start()
        wait_for(recv.at[t, others], back_send.at[t])
        load.wait()

        def store_pair(cols, total):
            recv[t, pl.ds(0, tok_dev), cols] = total.astype(jnp.bfloat16)

        weighted(t, 1, store_pair)
        pair_partial_copy(t).start()
        pair_partial_copy(t).wait_recv()
        weighted(t, 0, store)

    own.wait()
    dispatch(0, tok_ref)
    exchange(1)

    @pl.when(paired >= 2)
    def _():
        exchange(2)

    dispatch(1, zt.at[source(1)])

    @pl.when(paired < 2)
    def _():
        exchange(2)

    def reuse(t):
        wait_for(send.at[lax.rem(t, 2), others], send_sem.at[lax.rem(t, 2)])

    reuse(2)
    dispatch(2, zt.at[source(2)])
    for load in loads:
        load.wait()

    def middle(t, carry):
        exchange(t)
        expert(t - 2)
        reuse(t)
        dispatch(t, zt.at[source(t)])
        return carry

    lax.fori_loop(3, ex_count, middle, 0)

    def last(t, carry):
        expert(lax.rem(t, ex_count))
        return carry

    lax.fori_loop(ex_count - 2, ex_count + 1, last, 0)
    for slot in range(2):
        wait_for(send.at[slot, others], send_sem.at[slot])

    def home(t, carry):
        def store(cols, total):
            total = total + pret[t, :, cols].astype(jnp.float32)
            recv[t, pl.ds(tok_dev, tok_dev), cols] = total.astype(jnp.bfloat16)

        combined(t, store)
        plane_partial_copy(t).start()
        return carry

    lax.fori_loop(1, ex_count, home, 0)

    def finish(cols, total):
        total = total + pret[0, :, cols].astype(jnp.float32)
        out_ref[:, cols] = total.astype(jnp.bfloat16)

    def finish_all(cols, total):
        for d in range(1, ex_count):
            total = total + zret[d - 1, :, cols].astype(jnp.float32)
        finish(cols, total)

    for d in range(1, ex_count):
        wait_for(zret.at[d - 1], zret_recv.at[d])
    combined(0, finish_all)

    pair_token_copy(0, tok_ref).wait_send()
    pair_meta_copy(0).wait_send()
    pair_partial_copy(0).wait_send()
    sent_out(lambda copy: copy.wait_send())
    for d in range(1, ex_count):
        passed_on(source(d), lambda copy: copy.wait_send())
        meta_copy(d).wait_send()
        pair_token_copy(d, zt.at[source(d)]).wait_send()
        pair_meta_copy(d).wait_send()
        pair_partial_copy(d).wait_send()
        plane_partial_copy(d).wait_send()


def body(tokens, expert_ids, route_weight, w_gate, w_up, w_down):
    tok_dev, width = tokens.shape
    top_count = expert_ids.shape[1]
    ff = w_gate.shape[2]
    dp_count = lax.axis_size("dp")
    ex_count = lax.axis_size("expert")
    experts = dp_count * ex_count
    group = dp_count // 4
    needed = tok_dev * top_count * 3 // (2 * experts)
    cap = -(-needed // 16) * 16
    rows = dp_count * cap

    named = expert_ids.T[None, :, :] == jnp.arange(experts, dtype=jnp.int32)[:, None, None]
    chosen = jnp.any(named, axis=1)
    weight = jnp.sum(jnp.where(named, route_weight.T[None, :, :], 0.0), axis=1)
    index = jnp.arange(tok_dev, dtype=jnp.int32)
    before = (index[:, None] < index[None, :]).astype(jnp.bfloat16)
    slot = jnp.dot(chosen.astype(jnp.bfloat16), before, preferred_element_type=jnp.float32)
    slot = jnp.where(chosen, slot, -1.0)

    p = lax.axis_index("dp")
    c, b, a = p % group, (p // group) % 2, p // (2 * group)
    even = c % 2 == 0
    sides = []
    for side in range(2):
        for other in range(2):
            row = jnp.where(even, (a + other) % 2, (a + side) % 2)
            column = jnp.where(even, (b + side) % 2, (b + other) % 2)
            sides.append((row * 2 + column) * group + jnp.arange(group))
    order = jnp.concatenate(sides)

    def by_plane(v):
        v = v.reshape(dp_count, ex_count, tok_dev)[order]
        return v.reshape(2, 2 * group, ex_count, tok_dev).transpose(2, 0, 1, 3)

    meta = jnp.concatenate([by_plane(slot), by_plane(weight)], axis=2)

    any_space = pl.BlockSpec(memory_space=pl.ANY)
    vmem = pl.BlockSpec(memory_space=pltpu.VMEM)
    dma = pltpu.SemaphoreType.DMA
    each = dma((ex_count,))
    out, _, _, _ = pl.pallas_call(
        functools.partial(kernel, dp_count, ex_count, cap),
        out_shape=(
            jax.ShapeDtypeStruct((tok_dev, width), jnp.bfloat16),
            jax.ShapeDtypeStruct((ex_count, tok_dev, width), jnp.bfloat16),
            jax.ShapeDtypeStruct((ex_count, tok_dev, width), jnp.bfloat16),
            jax.ShapeDtypeStruct((ex_count, rows, width), jnp.bfloat16),
        ),
        in_specs=[any_space, any_space, any_space, any_space, any_space],
        out_specs=(vmem, any_space, any_space, any_space),
        scratch_shapes=[
            pltpu.VMEM((width, ff), jnp.bfloat16),
            pltpu.VMEM((width, ff), jnp.bfloat16),
            pltpu.VMEM((ff, width), jnp.bfloat16),
            pltpu.VMEM((ex_count, 2, 4 * group, tok_dev), jnp.float32),
            pltpu.VMEM((ex_count, 4 * group, tok_dev), jnp.float32),
            pltpu.VMEM((rows, 2 * tok_dev), jnp.bfloat16),
            pltpu.VMEM((2, rows, tok_dev), jnp.float32),
            pltpu.VMEM((2 * tok_dev, width), jnp.bfloat16),
            pltpu.VMEM((2, rows, width), jnp.bfloat16),
            pltpu.VMEM((ex_count, rows, width), jnp.bfloat16),
            pltpu.VMEM((rows, ff), jnp.bfloat16),
            pltpu.VMEM((ex_count, tok_dev, width), jnp.bfloat16),
            pltpu.VMEM((ex_count - 1, tok_dev, width), jnp.bfloat16),
            dma((3,)),
            dma((2,)),
            dma((ex_count + 1,)),
            each,
            each,
            each,
            each,
            each,
            each,
            each,
            dma((2,)),
            each,
            each,
            each,
            each,
            each,
            each,
            each,
        ],
        compiler_params=pltpu.CompilerParams(
            collective_id=0, has_side_effects=True, vmem_limit_bytes=60 * 1024 * 1024
        ),
        cost_estimate=pl.CostEstimate(
            flops=6 * ex_count * rows * width * ff,
            bytes_accessed=6 * width * ff + 6 * ex_count * rows * width,
            transcendentals=ex_count * rows * ff,
        ),
    )(tokens, meta, w_gate[0], w_up[0], w_down[0])
    return out


def solution(mesh):
    placed = (
        P(("dp", "expert"), None),
        P(("dp", "expert"), None),
        P(("dp", "expert"), None),
        P(("dp", "expert"), None, None),
        P(("dp", "expert"), None, None),
        P(("dp", "expert"), None, None),
    )
    return jax.shard_map(
        body, mesh=mesh, in_specs=placed, out_specs=P(("dp", "expert"), None), check_vma=False
    )
```

```python
import functools

import jax
import jax.numpy as jnp
from jax import lax
from jax.experimental import pallas as pl
from jax.experimental.pallas import tpu as pltpu
from jax.sharding import PartitionSpec as P

MESH = pl.DeviceIdType.MESH


def tile_of(extent, most):
    return most if extent % most == 0 else extent


def kernel(
    dp_count,
    ex_count,
    cap,
    tok_ref,
    meta_ref,
    wg_hbm,
    wu_hbm,
    wd_hbm,
    out_ref,
    zt,
    xt,
    ret,
    wg,
    wu,
    wd,
    zm,
    xm,
    pick,
    share,
    tok,
    send,
    recv,
    hid,
    pret,
    zret,
    weight_sem,
    local_sem,
    zt_send,
    zt_recv,
    zm_send,
    zm_recv,
    xt_send,
    xt_recv,
    xm_send,
    xm_recv,
    send_sem,
    recv_sem,
    back_send,
    back_recv,
    pret_send,
    pret_recv,
    zret_send,
    zret_recv,
):
    p = lax.axis_index("dp")
    z = lax.axis_index("expert")
    group = dp_count // 4
    c = p % group
    b = (p // group) % 2
    a = p // (2 * group)
    odd = c % 2

    def device(row, column, member):
        return (row * 2 + column) * group + member

    first = device(a + odd * (1 - 2 * a), b + (1 - odd) * (1 - 2 * b), c)
    row2, column2 = a + (1 - odd) * (1 - 2 * a), b + odd * (1 - 2 * b)
    width = tok_ref.shape[1]
    ff = wg.shape[1]
    tok_dev = tok_ref.shape[0]
    part = 2 * cap
    others = pl.ds(0, (2 * group - 1) * part)
    ff_tile = tile_of(ff, 256)
    col_tile = tile_of(width, 512)

    def section(i):
        return pl.ds(pl.multiple_of(i * part, part), part)

    loads = [
        pltpu.make_async_copy(src, dst, weight_sem.at[i])
        for i, (src, dst) in enumerate(((wg_hbm, wg), (wu_hbm, wu), (wd_hbm, wd)))
    ]
    own = pltpu.make_async_copy(tok_ref, tok.at[pl.ds(0, tok_dev)], local_sem.at[0])
    own.start()
    own_meta = pltpu.make_async_copy(meta_ref.at[z], zm.at[z], local_sem.at[1])
    own_meta.start()
    for load in loads:
        load.start()

    barrier = pltpu.get_barrier_semaphore()
    for d in range(1, dp_count):
        pl.semaphore_signal(barrier, inc=1, device_id=((p + d) % dp_count, z), device_id_type=MESH)
    for d in range(1, ex_count):
        pl.semaphore_signal(barrier, inc=1, device_id=(p, (z + d) % ex_count), device_id_type=MESH)
    pick[...] = jnp.zeros_like(pick)
    share[...] = jnp.zeros_like(share)
    pl.semaphore_wait(barrier, dp_count + ex_count - 2)

    def remote(src, dst, send_at, recv_at, target):
        return pltpu.make_async_remote_copy(
            src_ref=src,
            dst_ref=dst,
            send_sem=send_at,
            recv_sem=recv_at,
            device_id=target,
            device_id_type=MESH,
        )

    low_half = 2 * z <= ex_count - 1
    paired = jnp.where(low_half, 2 * z, 2 * (ex_count - 1 - z))

    def source(t):
        near = jnp.where(t % 2 == 1, z - (t + 1) // 2, z + t // 2)
        return jnp.where(t <= paired, near, jnp.where(low_half, t, ex_count - 1 - t))

    has_up, has_down = z + 1 < ex_count, z >= 1

    def up_copy(src, s):
        return remote(src, zt.at[s], zt_send.at[s], zt_recv.at[s], (p, (z + 1) % ex_count))

    def down_copy(src, s, at):
        target = (p, (z + ex_count - 1) % ex_count)
        return remote(src, zt.at[s], zt_send.at[at], zt_recv.at[s], target)

    def passed_on(s, act):
        @pl.when(jnp.logical_and(s < z, has_up))
        def _():
            act(up_copy(zt.at[s], s))

        @pl.when(jnp.logical_and(s > z, has_down))
        def _():
            act(down_copy(zt.at[s], s, s))

    def sent_out(act):
        @pl.when(has_up)
        def _():
            act(up_copy(tok_ref, z))

        @pl.when(has_down)
        def _():
            act(down_copy(tok_ref, z, ex_count))

    def meta_copy(d):
        target = (z + d) % ex_count
        return remote(meta_ref.at[target], zm.at[z], zm_send.at[d], zm_recv.at[z], (p, target))

    def pair_token_copy(t, src):
        return remote(src, xt.at[t], xt_send.at[t], xt_recv.at[t], (first, z))

    def pair_meta_copy(t):
        return remote(zm.at[source(t), 1], xm.at[t], xm_send.at[t], xm_recv.at[t], (first, z))

    def pair_partial_copy(t):
        return remote(
            recv.at[t, pl.ds(0, tok_dev)], pret.at[t], pret_send.at[t], pret_recv.at[t], (first, z)
        )

    def plane_partial_copy(t):
        s = source(t)
        away = (z + ex_count - s) % ex_count
        return remote(
            recv.at[t, pl.ds(tok_dev, tok_dev)],
            zret.at[away - 1],
            zret_send.at[t],
            zret_recv.at[away],
            (p, s),
        )

    def wait_for(ref, sem):
        pltpu.make_async_copy(ref, ref, sem).wait()

    sent_out(lambda copy: copy.start())
    pair_token_copy(0, tok_ref).start()
    for d in range(1, ex_count):
        meta_copy(d).start()
    own_meta.wait()
    pair_meta_copy(0).start()

    def exchange(t):
        s = source(t)
        wait_for(zm.at[s], zm_recv.at[s])
        pair_meta_copy(t).start()
        wait_for(zt.at[s], zt_recv.at[s])
        passed_on(s, lambda copy: copy.start())
        pair_token_copy(t, zt.at[s]).start()

    def one_hot(meta, dest, value):
        slots = lax.broadcasted_iota(jnp.int32, (cap, tok_dev), 0).astype(jnp.float32)
        return jnp.where(meta[dest : dest + 1, :] == slots, value, 0.0)

    def dispatch(t, src):
        load = pltpu.make_async_copy(src, tok.at[pl.ds(0, tok_dev)], local_sem.at[0])
        load.start()
        pair_meta_copy(t).wait_recv()
        for block, meta in enumerate((zm[source(t), 0], xm[t])):
            for dest in range(2 * group):
                rows = pl.ds((2 * dest + block) * cap, cap)
                hot = one_hot(meta, dest, 1.0).astype(jnp.bfloat16)
                pick[rows, pl.ds(block * tok_dev, tok_dev)] = hot
        pair_token_copy(t, src).wait_recv()
        pair = pltpu.make_async_copy(xt.at[t], tok.at[pl.ds(tok_dev, tok_dev)], local_sem.at[1])
        pair.start()
        load.wait()
        pair.wait()
        slot = lax.rem(t, 2)

        @pl.loop(0, width // col_tile)
        def _(i):
            cols = pl.ds(pl.multiple_of(i * col_tile, col_tile), col_tile)
            rows = jnp.dot(pick[...], tok[:, cols], preferred_element_type=jnp.float32)
            send[slot, :, cols] = rows.astype(jnp.bfloat16)

        def give(dest, at, target):
            remote(
                send.at[slot, section(dest)],
                recv.at[t, section(at)],
                send_sem.at[slot],
                recv_sem.at[t],
                (target, z),
            ).start()

        for member in range(group):
            give(group + member, group + c, device(row2, column2, member))
        for d in range(1, group):
            member = (c + d) % group
            give(member, c, device(a, b, member))
        keep = pltpu.make_async_copy(
            send.at[slot, section(c)], recv.at[t, section(c)], local_sem.at[0]
        )
        keep.start()
        keep.wait()

    def expert(t):
        wait_for(recv.at[t, others], recv_sem.at[t])

        @pl.loop(0, ff // ff_tile)
        def _(i):
            cols = pl.ds(pl.multiple_of(i * ff_tile, ff_tile), ff_tile)
            gate = jnp.dot(recv[t], wg[:, cols], preferred_element_type=jnp.float32)
            up = jnp.dot(recv[t], wu[:, cols], preferred_element_type=jnp.float32)
            hid[:, cols] = (gate / (1.0 + jnp.exp(-gate)) * up).astype(jnp.bfloat16)

        @pl.loop(0, width // col_tile)
        def _(i):
            cols = pl.ds(pl.multiple_of(i * col_tile, col_tile), col_tile)
            rows = jnp.dot(hid[...], wd[:, cols], preferred_element_type=jnp.float32)
            recv[t, :, cols] = rows.astype(jnp.bfloat16)

    def give_back_all(t):
        def give_back(at, dest, target):
            remote(
                recv.at[t, section(at)],
                ret.at[t, section(dest)],
                back_send.at[t],
                back_recv.at[t],
                (target, z),
            ).start()

        for member in range(group):
            target = device(1 - a, b, member) if member % 2 == 0 else device(a, 1 - b, member)
            give_back(group + member, group + c, target)
        for d in range(1, group):
            member = (c + d) % group
            give_back(member, c, device(a, b, member))
        keep = pltpu.make_async_copy(
            recv.at[t, section(c)], ret.at[t, section(c)], local_sem.at[0]
        )
        keep.start()
        keep.wait()

    def weighted(t, block, store):
        meta = xm[t] if block else zm[source(t), 0]
        for dest in range(2 * group):
            weight = meta[2 * group + dest : 2 * group + dest + 1, :]
            rows = pl.ds((2 * dest + block) * cap, cap)
            share[block, rows, :] = one_hot(meta, dest, weight)
        weight = share[block].T
        high = weight.astype(jnp.bfloat16)
        low = (weight - high.astype(jnp.float32)).astype(jnp.bfloat16)

        @pl.loop(0, width // col_tile)
        def _(i):
            cols = pl.ds(pl.multiple_of(i * col_tile, col_tile), col_tile)
            rows = send[lax.rem(t, 2), :, cols]
            total = jnp.dot(high, rows, preferred_element_type=jnp.float32)
            total = total + jnp.dot(low, rows, preferred_element_type=jnp.float32)
            store(cols, total)

    def left(t):
        wait_for(recv.at[t, others], back_send.at[t])

    def combine_pair(t):
        wait_for(ret.at[t, others], back_recv.at[t])
        load = pltpu.make_async_copy(ret.at[t], send.at[lax.rem(t, 2)], local_sem.at[0])
        load.start()
        load.wait()

        def store(cols, total):
            recv[t, pl.ds(0, tok_dev), cols] = total.astype(jnp.bfloat16)

        weighted(t, 1, store)
        pair_partial_copy(t).start()

    def combine_own(t):
        def store(cols, total):
            total = total + pret[t, :, cols].astype(jnp.float32)
            recv[t, pl.ds(tok_dev, tok_dev), cols] = total.astype(jnp.bfloat16)

        pair_partial_copy(t).wait_recv()
        weighted(t, 0, store)
        plane_partial_copy(t).start()

    own.wait()
    dispatch(0, tok_ref)
    exchange(1)

    @pl.when(paired >= 2)
    def _():
        exchange(2)

    dispatch(1, zt.at[source(1)])

    @pl.when(paired < 2)
    def _():
        exchange(2)

    def reuse(t):
        wait_for(send.at[lax.rem(t, 2), others], send_sem.at[lax.rem(t, 2)])

    reuse(2)
    dispatch(2, zt.at[source(2)])
    for load in loads:
        load.wait()

    def middle(t, carry):
        exchange(t)
        expert(t - 2)

        @pl.when(t > 3)
        def _():
            left(t - 3)

        give_back_all(t - 2)
        reuse(t)
        dispatch(t, zt.at[source(t)])
        return carry

    lax.fori_loop(3, ex_count, middle, 0)

    def last(i, carry):
        t = lax.rem(ex_count - 2 + i, ex_count)
        previous = ex_count - 3 + i
        expert(t)
        left(previous)
        give_back_all(t)

        @pl.when(i == 0)
        def _():
            for slot in range(2):
                wait_for(send.at[slot, others], send_sem.at[slot])

        def back(q, carry):
            combine_pair(q)

            @pl.when(q > 1)
            def _():
                combine_own(q - 1)

            return carry

        lax.fori_loop(jnp.where(i == 0, 1, previous), previous + 1, back, 0)
        return carry

    lax.fori_loop(0, 3, last, 0)
    left(0)
    combine_pair(0)
    combine_own(ex_count - 1)

    def finish(cols, total):
        total = total + pret[0, :, cols].astype(jnp.float32)
        for d in range(1, ex_count):
            total = total + zret[d - 1, :, cols].astype(jnp.float32)
        out_ref[:, cols] = total.astype(jnp.bfloat16)

    pair_partial_copy(0).wait_recv()
    for d in range(1, ex_count):
        wait_for(zret.at[d - 1], zret_recv.at[d])
    weighted(0, 0, finish)

    pair_token_copy(0, tok_ref).wait_send()
    pair_meta_copy(0).wait_send()
    pair_partial_copy(0).wait_send()
    sent_out(lambda copy: copy.wait_send())
    for d in range(1, ex_count):
        passed_on(source(d), lambda copy: copy.wait_send())
        meta_copy(d).wait_send()
        pair_token_copy(d, zt.at[source(d)]).wait_send()
        pair_meta_copy(d).wait_send()
        pair_partial_copy(d).wait_send()
        plane_partial_copy(d).wait_send()


def body(tokens, expert_ids, route_weight, w_gate, w_up, w_down):
    tok_dev, width = tokens.shape
    top_count = expert_ids.shape[1]
    ff = w_gate.shape[2]
    dp_count = lax.axis_size("dp")
    ex_count = lax.axis_size("expert")
    experts = dp_count * ex_count
    group = dp_count // 4
    needed = tok_dev * top_count * 3 // (2 * experts)
    cap = -(-needed // 16) * 16
    rows = dp_count * cap

    named = expert_ids.T[None, :, :] == jnp.arange(experts, dtype=jnp.int32)[:, None, None]
    chosen = jnp.any(named, axis=1)
    weight = jnp.sum(jnp.where(named, route_weight.T[None, :, :], 0.0), axis=1)
    index = jnp.arange(tok_dev, dtype=jnp.int32)
    before = (index[:, None] < index[None, :]).astype(jnp.bfloat16)
    slot = jnp.dot(chosen.astype(jnp.bfloat16), before, preferred_element_type=jnp.float32)
    slot = jnp.where(chosen, slot, -1.0)

    p = lax.axis_index("dp")
    c, b, a = p % group, (p // group) % 2, p // (2 * group)
    even = c % 2 == 0
    sides = []
    for side in range(2):
        for other in range(2):
            row = jnp.where(even, (a + other) % 2, (a + side) % 2)
            column = jnp.where(even, (b + side) % 2, (b + other) % 2)
            sides.append((row * 2 + column) * group + jnp.arange(group))
    order = jnp.concatenate(sides)

    def by_plane(v):
        v = v.reshape(dp_count, ex_count, tok_dev)[order]
        return v.reshape(2, 2 * group, ex_count, tok_dev).transpose(2, 0, 1, 3)

    meta = jnp.concatenate([by_plane(slot), by_plane(weight)], axis=2)

    any_space = pl.BlockSpec(memory_space=pl.ANY)
    vmem = pl.BlockSpec(memory_space=pltpu.VMEM)
    dma = pltpu.SemaphoreType.DMA
    each = dma((ex_count,))
    out, _, _, _ = pl.pallas_call(
        functools.partial(kernel, dp_count, ex_count, cap),
        out_shape=(
            jax.ShapeDtypeStruct((tok_dev, width), jnp.bfloat16),
            jax.ShapeDtypeStruct((ex_count, tok_dev, width), jnp.bfloat16),
            jax.ShapeDtypeStruct((ex_count, tok_dev, width), jnp.bfloat16),
            jax.ShapeDtypeStruct((ex_count, rows, width), jnp.bfloat16),
        ),
        in_specs=[any_space, any_space, any_space, any_space, any_space],
        out_specs=(vmem, any_space, any_space, any_space),
        scratch_shapes=[
            pltpu.VMEM((width, ff), jnp.bfloat16),
            pltpu.VMEM((width, ff), jnp.bfloat16),
            pltpu.VMEM((ff, width), jnp.bfloat16),
            pltpu.VMEM((ex_count, 2, 4 * group, tok_dev), jnp.float32),
            pltpu.VMEM((ex_count, 4 * group, tok_dev), jnp.float32),
            pltpu.VMEM((rows, 2 * tok_dev), jnp.bfloat16),
            pltpu.VMEM((2, rows, tok_dev), jnp.float32),
            pltpu.VMEM((2 * tok_dev, width), jnp.bfloat16),
            pltpu.VMEM((2, rows, width), jnp.bfloat16),
            pltpu.VMEM((ex_count, rows, width), jnp.bfloat16),
            pltpu.VMEM((rows, ff), jnp.bfloat16),
            pltpu.VMEM((ex_count, tok_dev, width), jnp.bfloat16),
            pltpu.VMEM((ex_count - 1, tok_dev, width), jnp.bfloat16),
            dma((3,)),
            dma((2,)),
            dma((ex_count + 1,)),
            each,
            each,
            each,
            each,
            each,
            each,
            each,
            dma((2,)),
            each,
            each,
            each,
            each,
            each,
            each,
            each,
        ],
        compiler_params=pltpu.CompilerParams(
            collective_id=0, has_side_effects=True, vmem_limit_bytes=60 * 1024 * 1024
        ),
        cost_estimate=pl.CostEstimate(
            flops=6 * ex_count * rows * width * ff,
            bytes_accessed=6 * width * ff + 6 * ex_count * rows * width,
            transcendentals=ex_count * rows * ff,
        ),
    )(tokens, meta, w_gate[0], w_up[0], w_down[0])
    return out


def solution(mesh):
    placed = (
        P(("dp", "expert"), None),
        P(("dp", "expert"), None),
        P(("dp", "expert"), None),
        P(("dp", "expert"), None, None),
        P(("dp", "expert"), None, None),
        P(("dp", "expert"), None, None),
    )
    return jax.shard_map(
        body, mesh=mesh, in_specs=placed, out_specs=P(("dp", "expert"), None), check_vma=False
    )
```

```python
import functools

import jax
import jax.numpy as jnp
from jax import lax
from jax.experimental import pallas as pl
from jax.experimental.pallas import tpu as pltpu
from jax.sharding import PartitionSpec as P

MESH = pl.DeviceIdType.MESH


def tile_of(extent, most):
    return most if extent % most == 0 else extent


def kernel(
    dp_count,
    ex_count,
    cap,
    tok_ref,
    meta_ref,
    wg_hbm,
    wu_hbm,
    wd_hbm,
    out_ref,
    zt,
    xt,
    ret,
    wg,
    wu,
    wd,
    zm,
    xm,
    pick,
    share,
    tok,
    send,
    recv,
    hid,
    pret,
    zret,
    weight_sem,
    local_sem,
    zt_send,
    zt_recv,
    zm_send,
    zm_recv,
    xt_send,
    xt_recv,
    xm_send,
    xm_recv,
    send_sem,
    recv_sem,
    back_send,
    back_recv,
    pret_send,
    pret_recv,
    zret_send,
    zret_recv,
):
    p = lax.axis_index("dp")
    z = lax.axis_index("expert")
    group = dp_count // 4
    c = p % group
    b = (p // group) % 2
    a = p // (2 * group)
    odd = c % 2

    def device(row, column, member):
        return (row * 2 + column) * group + member

    first = device(a + odd * (1 - 2 * a), b + (1 - odd) * (1 - 2 * b), c)
    row2, column2 = a + (1 - odd) * (1 - 2 * a), b + odd * (1 - 2 * b)
    width = tok_ref.shape[1]
    ff = wg.shape[1]
    tok_dev = tok_ref.shape[0]
    part = 2 * cap
    others = pl.ds(0, (2 * group - 1) * part)
    ff_tile = tile_of(ff, 256)
    col_tile = tile_of(width, 512)

    def section(i):
        return pl.ds(pl.multiple_of(i * part, part), part)

    loads = [
        pltpu.make_async_copy(src, dst, weight_sem.at[i])
        for i, (src, dst) in enumerate(((wg_hbm, wg), (wu_hbm, wu), (wd_hbm, wd)))
    ]
    own = pltpu.make_async_copy(tok_ref, tok.at[pl.ds(0, tok_dev)], local_sem.at[0])
    own.start()
    own_meta = pltpu.make_async_copy(meta_ref.at[z], zm.at[z], local_sem.at[1])
    own_meta.start()
    for load in loads:
        load.start()

    barrier = pltpu.get_barrier_semaphore()
    for d in range(1, dp_count):
        pl.semaphore_signal(barrier, inc=1, device_id=((p + d) % dp_count, z), device_id_type=MESH)
    for d in range(1, ex_count):
        pl.semaphore_signal(barrier, inc=1, device_id=(p, (z + d) % ex_count), device_id_type=MESH)
    pick[...] = jnp.zeros_like(pick)
    share[...] = jnp.zeros_like(share)
    pl.semaphore_wait(barrier, dp_count + ex_count - 2)

    def remote(src, dst, send_at, recv_at, target):
        return pltpu.make_async_remote_copy(
            src_ref=src,
            dst_ref=dst,
            send_sem=send_at,
            recv_sem=recv_at,
            device_id=target,
            device_id_type=MESH,
        )

    low_half = 2 * z <= ex_count - 1
    paired = jnp.where(low_half, 2 * z, 2 * (ex_count - 1 - z))

    def source(t):
        inward = jnp.where(low_half, 1, -1)
        near = z + inward * jnp.where(t % 2 == 1, (t + 1) // 2, -(t // 2))
        return jnp.where(t <= paired, near, jnp.where(low_half, t, ex_count - 1 - t))

    has_up, has_down = z + 1 < ex_count, z >= 1

    def up_copy(src, s):
        return remote(src, zt.at[s], zt_send.at[s], zt_recv.at[s], (p, (z + 1) % ex_count))

    def down_copy(src, s, at):
        target = (p, (z + ex_count - 1) % ex_count)
        return remote(src, zt.at[s], zt_send.at[at], zt_recv.at[s], target)

    def passed_on(s, act):
        @pl.when(jnp.logical_and(s < z, has_up))
        def _():
            act(up_copy(zt.at[s], s))

        @pl.when(jnp.logical_and(s > z, has_down))
        def _():
            act(down_copy(zt.at[s], s, s))

    def sent_out(act):
        @pl.when(has_up)
        def _():
            act(up_copy(tok_ref, z))

        @pl.when(has_down)
        def _():
            act(down_copy(tok_ref, z, ex_count))

    def meta_copy(d):
        target = (z + d) % ex_count
        return remote(meta_ref.at[target], zm.at[z], zm_send.at[d], zm_recv.at[z], (p, target))

    def pair_token_copy(t, src):
        return remote(src, xt.at[t], xt_send.at[t], xt_recv.at[t], (first, z))

    def pair_meta_copy(t):
        return remote(zm.at[source(t), 1], xm.at[t], xm_send.at[t], xm_recv.at[t], (first, z))

    def pair_partial_copy(t):
        return remote(
            recv.at[t, pl.ds(0, tok_dev)], pret.at[t], pret_send.at[t], pret_recv.at[t], (first, z)
        )

    def plane_partial_copy(t):
        s = source(t)
        away = (z + ex_count - s) % ex_count
        return remote(
            recv.at[t, pl.ds(tok_dev, tok_dev)],
            zret.at[away - 1],
            zret_send.at[t],
            zret_recv.at[away],
            (p, s),
        )

    def wait_for(ref, sem):
        pltpu.make_async_copy(ref, ref, sem).wait()

    sent_out(lambda copy: copy.start())
    pair_token_copy(0, tok_ref).start()
    for d in range(1, ex_count):
        meta_copy(d).start()
    own_meta.wait()
    pair_meta_copy(0).start()

    def exchange(t):
        s = source(t)
        wait_for(zm.at[s], zm_recv.at[s])
        pair_meta_copy(t).start()
        wait_for(zt.at[s], zt_recv.at[s])
        passed_on(s, lambda copy: copy.start())
        pair_token_copy(t, zt.at[s]).start()

    def one_hot(meta, dest, value):
        slots = lax.broadcasted_iota(jnp.int32, (cap, tok_dev), 0).astype(jnp.float32)
        return jnp.where(meta[dest : dest + 1, :] == slots, value, 0.0)

    def dispatch(t, src):
        load = pltpu.make_async_copy(src, tok.at[pl.ds(0, tok_dev)], local_sem.at[0])
        load.start()
        pair_meta_copy(t).wait_recv()
        for block, meta in enumerate((zm[source(t), 0], xm[t])):
            for dest in range(2 * group):
                rows = pl.ds((2 * dest + block) * cap, cap)
                hot = one_hot(meta, dest, 1.0).astype(jnp.bfloat16)
                pick[rows, pl.ds(block * tok_dev, tok_dev)] = hot
        pair_token_copy(t, src).wait_recv()
        pair = pltpu.make_async_copy(xt.at[t], tok.at[pl.ds(tok_dev, tok_dev)], local_sem.at[1])
        pair.start()
        load.wait()
        pair.wait()
        slot = lax.rem(t, 2)

        @pl.loop(0, width // col_tile)
        def _(i):
            cols = pl.ds(pl.multiple_of(i * col_tile, col_tile), col_tile)
            rows = jnp.dot(pick[...], tok[:, cols], preferred_element_type=jnp.float32)
            send[slot, :, cols] = rows.astype(jnp.bfloat16)

        def give(dest, at, target):
            remote(
                send.at[slot, section(dest)],
                recv.at[t, section(at)],
                send_sem.at[slot],
                recv_sem.at[t],
                (target, z),
            ).start()

        for member in range(group):
            give(group + member, group + c, device(row2, column2, member))
        for d in range(1, group):
            member = (c + d) % group
            give(member, c, device(a, b, member))
        keep = pltpu.make_async_copy(
            send.at[slot, section(c)], recv.at[t, section(c)], local_sem.at[0]
        )
        keep.start()
        keep.wait()

    def expert(t):
        wait_for(recv.at[t, others], recv_sem.at[t])

        @pl.loop(0, ff // ff_tile)
        def _(i):
            cols = pl.ds(pl.multiple_of(i * ff_tile, ff_tile), ff_tile)
            gate = jnp.dot(recv[t], wg[:, cols], preferred_element_type=jnp.float32)
            up = jnp.dot(recv[t], wu[:, cols], preferred_element_type=jnp.float32)
            hid[:, cols] = (gate / (1.0 + jnp.exp(-gate)) * up).astype(jnp.bfloat16)

        @pl.loop(0, width // col_tile)
        def _(i):
            cols = pl.ds(pl.multiple_of(i * col_tile, col_tile), col_tile)
            rows = jnp.dot(hid[...], wd[:, cols], preferred_element_type=jnp.float32)
            recv[t, :, cols] = rows.astype(jnp.bfloat16)

    def give_back_all(t):
        def give_back(at, dest, target):
            remote(
                recv.at[t, section(at)],
                ret.at[t, section(dest)],
                back_send.at[t],
                back_recv.at[t],
                (target, z),
            ).start()

        for member in range(group):
            target = device(1 - a, b, member) if member % 2 == 0 else device(a, 1 - b, member)
            give_back(group + member, group + c, target)
        for d in range(1, group):
            member = (c + d) % group
            give_back(member, c, device(a, b, member))
        keep = pltpu.make_async_copy(
            recv.at[t, section(c)], ret.at[t, section(c)], local_sem.at[0]
        )
        keep.start()
        keep.wait()

    def weighted(t, block, store):
        meta = xm[t] if block else zm[source(t), 0]
        for dest in range(2 * group):
            weight = meta[2 * group + dest : 2 * group + dest + 1, :]
            rows = pl.ds((2 * dest + block) * cap, cap)
            share[block, rows, :] = one_hot(meta, dest, weight)
        weight = share[block].T
        high = weight.astype(jnp.bfloat16)
        low = (weight - high.astype(jnp.float32)).astype(jnp.bfloat16)

        @pl.loop(0, width // col_tile)
        def _(i):
            cols = pl.ds(pl.multiple_of(i * col_tile, col_tile), col_tile)
            rows = send[lax.rem(t, 2), :, cols]
            total = jnp.dot(high, rows, preferred_element_type=jnp.float32)
            total = total + jnp.dot(low, rows, preferred_element_type=jnp.float32)
            store(cols, total)

    def left(t):
        wait_for(recv.at[t, others], back_send.at[t])

    def combine_pair(t):
        wait_for(ret.at[t, others], back_recv.at[t])
        load = pltpu.make_async_copy(ret.at[t], send.at[lax.rem(t, 2)], local_sem.at[0])
        load.start()
        load.wait()

        def store(cols, total):
            recv[t, pl.ds(0, tok_dev), cols] = total.astype(jnp.bfloat16)

        weighted(t, 1, store)
        pair_partial_copy(t).start()

    def combine_own(t):
        def store(cols, total):
            total = total + pret[t, :, cols].astype(jnp.float32)
            recv[t, pl.ds(tok_dev, tok_dev), cols] = total.astype(jnp.bfloat16)

        pair_partial_copy(t).wait_recv()
        weighted(t, 0, store)
        plane_partial_copy(t).start()

    own.wait()
    dispatch(0, tok_ref)
    exchange(1)

    @pl.when(paired >= 2)
    def _():
        exchange(2)

    dispatch(1, zt.at[source(1)])

    @pl.when(paired < 2)
    def _():
        exchange(2)

    def reuse(t):
        wait_for(send.at[lax.rem(t, 2), others], send_sem.at[lax.rem(t, 2)])

    reuse(2)
    dispatch(2, zt.at[source(2)])
    for load in loads:
        load.wait()

    def middle(t, carry):
        exchange(t)
        expert(t - 2)

        @pl.when(t > 3)
        def _():
            left(t - 3)

        give_back_all(t - 2)
        reuse(t)
        dispatch(t, zt.at[source(t)])
        return carry

    lax.fori_loop(3, ex_count, middle, 0)

    def last(i, carry):
        t = lax.rem(ex_count - 2 + i, ex_count)
        previous = ex_count - 3 + i
        expert(t)
        left(previous)
        give_back_all(t)

        @pl.when(i == 0)
        def _():
            for slot in range(2):
                wait_for(send.at[slot, others], send_sem.at[slot])

        def back(q, carry):
            combine_pair(q)

            @pl.when(q > 1)
            def _():
                combine_own(q - 1)

            return carry

        lax.fori_loop(jnp.where(i == 0, 1, previous), previous + 1, back, 0)
        return carry

    lax.fori_loop(0, 3, last, 0)
    left(0)
    combine_pair(0)
    combine_own(ex_count - 1)

    def finish(cols, total):
        total = total + pret[0, :, cols].astype(jnp.float32)
        for d in range(1, ex_count):
            total = total + zret[d - 1, :, cols].astype(jnp.float32)
        out_ref[:, cols] = total.astype(jnp.bfloat16)

    pair_partial_copy(0).wait_recv()
    for d in range(1, ex_count):
        wait_for(zret.at[d - 1], zret_recv.at[d])
    weighted(0, 0, finish)

    pair_token_copy(0, tok_ref).wait_send()
    pair_meta_copy(0).wait_send()
    pair_partial_copy(0).wait_send()
    sent_out(lambda copy: copy.wait_send())
    for d in range(1, ex_count):
        passed_on(source(d), lambda copy: copy.wait_send())
        meta_copy(d).wait_send()
        pair_token_copy(d, zt.at[source(d)]).wait_send()
        pair_meta_copy(d).wait_send()
        pair_partial_copy(d).wait_send()
        plane_partial_copy(d).wait_send()


def body(tokens, expert_ids, route_weight, w_gate, w_up, w_down):
    tok_dev, width = tokens.shape
    top_count = expert_ids.shape[1]
    ff = w_gate.shape[2]
    dp_count = lax.axis_size("dp")
    ex_count = lax.axis_size("expert")
    experts = dp_count * ex_count
    group = dp_count // 4
    needed = tok_dev * top_count * 3 // (2 * experts)
    cap = -(-needed // 16) * 16
    rows = dp_count * cap

    named = expert_ids.T[None, :, :] == jnp.arange(experts, dtype=jnp.int32)[:, None, None]
    chosen = jnp.any(named, axis=1)
    weight = jnp.sum(jnp.where(named, route_weight.T[None, :, :], 0.0), axis=1)
    index = jnp.arange(tok_dev, dtype=jnp.int32)
    before = (index[:, None] < index[None, :]).astype(jnp.bfloat16)
    slot = jnp.dot(chosen.astype(jnp.bfloat16), before, preferred_element_type=jnp.float32)
    slot = jnp.where(chosen, slot, -1.0)

    p = lax.axis_index("dp")
    c, b, a = p % group, (p // group) % 2, p // (2 * group)
    even = c % 2 == 0
    sides = []
    for side in range(2):
        for other in range(2):
            row = jnp.where(even, (a + other) % 2, (a + side) % 2)
            column = jnp.where(even, (b + side) % 2, (b + other) % 2)
            sides.append((row * 2 + column) * group + jnp.arange(group))
    order = jnp.concatenate(sides)

    def by_plane(v):
        v = v.reshape(dp_count, ex_count, tok_dev)[order]
        return v.reshape(2, 2 * group, ex_count, tok_dev).transpose(2, 0, 1, 3)

    meta = jnp.concatenate([by_plane(slot), by_plane(weight)], axis=2)

    any_space = pl.BlockSpec(memory_space=pl.ANY)
    vmem = pl.BlockSpec(memory_space=pltpu.VMEM)
    dma = pltpu.SemaphoreType.DMA
    each = dma((ex_count,))
    out, _, _, _ = pl.pallas_call(
        functools.partial(kernel, dp_count, ex_count, cap),
        out_shape=(
            jax.ShapeDtypeStruct((tok_dev, width), jnp.bfloat16),
            jax.ShapeDtypeStruct((ex_count, tok_dev, width), jnp.bfloat16),
            jax.ShapeDtypeStruct((ex_count, tok_dev, width), jnp.bfloat16),
            jax.ShapeDtypeStruct((ex_count, rows, width), jnp.bfloat16),
        ),
        in_specs=[any_space, any_space, any_space, any_space, any_space],
        out_specs=(vmem, any_space, any_space, any_space),
        scratch_shapes=[
            pltpu.VMEM((width, ff), jnp.bfloat16),
            pltpu.VMEM((width, ff), jnp.bfloat16),
            pltpu.VMEM((ff, width), jnp.bfloat16),
            pltpu.VMEM((ex_count, 2, 4 * group, tok_dev), jnp.float32),
            pltpu.VMEM((ex_count, 4 * group, tok_dev), jnp.float32),
            pltpu.VMEM((rows, 2 * tok_dev), jnp.bfloat16),
            pltpu.VMEM((2, rows, tok_dev), jnp.float32),
            pltpu.VMEM((2 * tok_dev, width), jnp.bfloat16),
            pltpu.VMEM((2, rows, width), jnp.bfloat16),
            pltpu.VMEM((ex_count, rows, width), jnp.bfloat16),
            pltpu.VMEM((rows, ff), jnp.bfloat16),
            pltpu.VMEM((ex_count, tok_dev, width), jnp.bfloat16),
            pltpu.VMEM((ex_count - 1, tok_dev, width), jnp.bfloat16),
            dma((3,)),
            dma((2,)),
            dma((ex_count + 1,)),
            each,
            each,
            each,
            each,
            each,
            each,
            each,
            dma((2,)),
            each,
            each,
            each,
            each,
            each,
            each,
            each,
        ],
        compiler_params=pltpu.CompilerParams(
            collective_id=0, has_side_effects=True, vmem_limit_bytes=60 * 1024 * 1024
        ),
        cost_estimate=pl.CostEstimate(
            flops=6 * ex_count * rows * width * ff,
            bytes_accessed=6 * width * ff + 6 * ex_count * rows * width,
            transcendentals=ex_count * rows * ff,
        ),
    )(tokens, meta, w_gate[0], w_up[0], w_down[0])
    return out


def solution(mesh):
    placed = (
        P(("dp", "expert"), None),
        P(("dp", "expert"), None),
        P(("dp", "expert"), None),
        P(("dp", "expert"), None, None),
        P(("dp", "expert"), None, None),
        P(("dp", "expert"), None, None),
    )
    return jax.shard_map(
        body, mesh=mesh, in_specs=placed, out_specs=P(("dp", "expert"), None), check_vma=False
    )
```
